32 devices in a mesh: fac: 8 (over y, x, core), loc: 4 (over z).
Axes of the slice: x: 2, y: 2, z: 4, core: 2. Of those that a mesh axis runs over, the one named last changes fastest.
Arguments:
- quad_cost: float32 [128, 128, 128, 128], P('fac', 'loc'), may hold values from -30 to 30
- leader: float32 [128, 128], P('fac', 'loc'), may hold values from -4 to 4
Outputs:
- new_cost: float32 [128, 128, 128, 128], P('fac', 'loc')
- new_leader: float32 [128, 128], P('fac', 'loc')
The draws below stay inside these ranges and needn't reach their ends.
All inputs are finite; a program needn't handle non-finite values.
Results may differ from the reference program's by a relative error of at most 0.0001.
Values sent between devices are 32-bit elements; how exact they have to be, the bound alone decides.
A program may use at most 448 MiB of HBM per device.

```python
import math
import jax
import jax.numpy as jnp
from jax import lax

N = 128
SWEEPS = 3
UPDATES = 1


def draw_quad_cost(key, part):
    key_base = jax.random.fold_in(key, 101)
    key_row = jax.random.fold_in(key, 103)
    key_col = jax.random.fold_in(key, 104)
    base = jnp.clip(jax.random.normal(key_base, (N, N, N, N), jnp.float32), -4.0, 4.0)
    row_scale = jnp.exp(jax.random.uniform(key_row, (N, N, N, 1), jnp.float32, 0.0, math.log(3.0)))
    col_scale = jnp.exp(jax.random.uniform(key_col, (N, N, 1, N), jnp.float32, 0.0, math.log(2.0)))
    return base * row_scale * col_scale


def levels(rng, shape, pieces, low, high):
    gain, own = 1.0, jax.random.fold_in(rng, 6)
    for axis_at, blocks in pieces:
        steps = jnp.exp(jax.random.uniform(jax.random.fold_in(own, axis_at), (blocks,), jnp.float32, low / len(pieces), high / len(pieces)))
        gain = gain * jnp.repeat(steps, shape[axis_at] // blocks).reshape([-1 if axis == axis_at else 1 for axis in range(len(shape))])
    return gain


def scatter_about(key, dims, deviation, reach, pieces=(), held_as=jnp.bfloat16):
    result = deviation * jax.random.normal(key, dims, jnp.float32)
    if pieces:
        result = result * levels(key, dims, pieces, -0.22, 0.18)
    return jnp.clip(result, -reach, reach).astype(held_as)


def setup_inputs(seed: int = 0) -> dict:
    streams_of = jax.random.split(jax.random.key(seed), 3)
    return {
        "quad_cost": draw_quad_cost(jax.random.fold_in(streams_of[2], 71), 0),
        "leader": scatter_about(streams_of[1], (N, N), 1.0, 4.0, ((0, 8), (1, 4)), jnp.float32),
    }


temper = 0.15
leader_temper = 0.1


def soft_min(values, axis, scale):
    scaled = -values / scale
    highest = jnp.max(scaled, axis=axis, keepdims=True)
    totals = jnp.sum(jnp.exp(scaled - highest), axis=axis, keepdims=True)
    return jnp.squeeze(-scale * (highest + jnp.log(totals)), axis)


def sweep_block(block):
    col_dual = jnp.zeros(block.shape[:-2] + (block.shape[-1],), jnp.float32)
    row_dual = jnp.zeros(block.shape[:-1], jnp.float32)
    for sweep in range(SWEEPS):
        row_dual = soft_min(block - col_dual[..., None, :], -1, temper)
        col_dual = soft_min(block - row_dual[..., :, None], -2, temper)
    reduced = block - row_dual[..., :, None] - col_dual[..., None, :]
    worth = (jnp.sum(row_dual, -1) + jnp.sum(col_dual, -1)) / N
    return reduced, worth


def reference(quad_cost, leader):
    for update in range(UPDATES):
        reduced, worth = lax.map(sweep_block, quad_cost)
        partner = jnp.transpose(reduced, (2, 3, 0, 1))
        quad_cost = 0.5 * (reduced + partner)
        leader = leader + worth
        leader = leader - soft_min(leader, 1, leader_temper)[:, None]
        leader = leader - soft_min(leader, 0, leader_temper)[None, :]
    return quad_cost, leader
```

```python
import functools
import math

import jax
import jax.numpy as jnp
from jax import lax
from jax.experimental import pallas as pl
from jax.experimental.pallas import tpu as pltpu
from jax.sharding import PartitionSpec as P

SWEEPS = 3

temper = 0.15
leader_temper = 0.1

SCALE = 1.0 / (temper * math.log(2.0))
LOG2E = 1.0 / math.log(2.0)
GROUP = 8


def combined_all(x, axis, combine):
    everything = jax.tree.map(lambda part: lax.all_gather(part, axis), x)
    initial = jax.tree.map(lambda part: part[0], everything)

    def hop(k, so_far):
        return combine(so_far, jax.tree.map(lambda part: part[k], everything))

    return lax.fori_loop(1, lax.axis_size(axis), hop, initial)


def partial_totals(values, axis):
    scaled = -values / leader_temper
    highest = jnp.max(scaled, axis=axis)
    totals = jnp.sum(jnp.exp(scaled - jnp.expand_dims(highest, axis)), axis=axis)
    return (highest, totals)


def join_totals(first, second):
    highest = jnp.maximum(first[0], second[0])
    totals = first[1] * jnp.exp(first[0] - highest) + second[1] * jnp.exp(second[0] - highest)
    return (highest, totals)


def swap_lane_groups(rows, width):
    rows = list(rows)
    count = len(rows)
    lane_group = lax.broadcasted_iota(jnp.int32, rows[0].shape, 1) // width
    lanes = rows[0].shape[1]
    dist = count // 2
    while dist:
        low = (lane_group // dist) % 2 == 0
        for r in range(count):
            if (r // dist) % 2 == 0:
                a, b = rows[r], rows[r + dist]
                rows[r] = jnp.where(low, a, pltpu.roll(b, dist * width, 1))
                rows[r + dist] = jnp.where(low, pltpu.roll(a, lanes - dist * width, 1), b)
        dist //= 2
    return rows


def sweep_kernel(loc_count, with_prior, *refs):
    if with_prior:
        c_ref, _, r_ref, send_ref, w_ref, p_s, z_s = refs
    else:
        c_ref, r_ref, send_ref, w_ref, p_s, z_s = refs
    n = c_ref.shape[1]
    width = n // loc_count
    per_fac = send_ref.shape[3]
    batch = 64
    shape = (GROUP, n)

    zero = jnp.zeros(shape, jnp.float32)

    def first_rows(step, top_and_sum):
        top, u_sum = top_and_sum
        k0 = step * batch
        ys = [c_ref[pl.ds(k0 + t, GROUP, stride=n), :] * (-SCALE) for t in range(batch)]
        highs = [jnp.max(y, axis=1, keepdims=True) for y in ys]
        sums = [jnp.sum(jnp.exp2(y - h), axis=1, keepdims=True) for y, h in zip(ys, highs)]
        us = [-(h + jnp.log(s) * LOG2E) for h, s in zip(highs, sums)]
        for t in range(batch):
            z = ys[t] + us[t]
            z_s[k0 + t] = z
            top = jnp.maximum(top, z)
            u_sum = u_sum + us[t]
        return top, u_sum

    top, u_sum = lax.fori_loop(
        0, n // batch, first_rows,
        (jnp.full(shape, -jnp.inf, jnp.float32), jnp.zeros((GROUP, 1), jnp.float32)),
    )

    def first_columns(step, totals):
        k0 = step * batch
        totals = list(totals)
        for t in range(batch):
            e = jnp.exp2(z_s[k0 + t] - top)
            p_s[k0 + t] = e
            totals[t % 4] = totals[t % 4] + e
        return tuple(totals)

    totals = lax.fori_loop(0, n // batch, first_columns, (zero,) * 4)
    total = (totals[0] + totals[1]) + (totals[2] + totals[3])

    weight = 1.0 / total
    for sweep in range(1, SWEEPS):
        last = sweep == SWEEPS - 1

        def later(step, totals, weight=weight, last=last):
            k0 = step * batch
            totals = list(totals)
            ps = [p_s[k0 + t] for t in range(batch)]
            sums = [jnp.sum(p * weight, axis=1, keepdims=True) for p in ps]
            for t in range(batch):
                totals[t % 4] = totals[t % 4] + ps[t] * (1.0 / sums[t])
            if last:
                for t in range(batch):
                    drop = jnp.log(sums[t]) * LOG2E
                    z_s[k0 + t] = z_s[k0 + t] - drop
                    totals[4] = totals[4] - drop
            return tuple(totals)

        start = (zero,) * 4 + ((u_sum,) if last else ())
        totals = lax.fori_loop(0, n // batch, later, start)
        total = (totals[0] + totals[1]) + (totals[2] + totals[3])
        weight = 1.0 / total
        if last:
            u_sum = totals[4]
    col = -(top + jnp.log(total) * LOG2E)

    worth = (u_sum + jnp.sum(col, axis=1, keepdims=True)) * (1.0 / (SCALE * n))
    w_ref[0] = jnp.broadcast_to(worth, shape)

    def finish(q, carry):
        k0 = q * loc_count
        outs = []
        for t in range(loc_count):
            r = (z_s[k0 + t] + col) * (-1.0 / SCALE)
            r_ref[pl.ds(k0 + t, GROUP, stride=n), :] = r
            outs.append(r)
        for b, packed in enumerate(swap_lane_groups(outs, width)):
            send_ref[q // per_fac, b, 0, q % per_fac] = packed
        return carry

    lax.fori_loop(0, n // loc_count, finish, 0, unroll=2)


def sweep_chunk(cost, prior, start, size, fac_rows, loc_rows, fac_count, loc_count):
    n = cost.shape[1]
    groups = loc_rows // GROUP
    per_fac = fac_rows // loc_count
    rows = GROUP * n
    elements = size * loc_rows * n * n
    in_specs = [pl.BlockSpec((rows, n), lambda i, g: ((i + start) * groups + g, 0))]
    operands = [cost]
    aliases = {}
    if prior is not None:
        in_specs.append(pl.BlockSpec(memory_space=pl.ANY))
        operands.append(prior)
        aliases = {1: 0}
    return pl.pallas_call(
        functools.partial(sweep_kernel, loc_count, prior is not None),
        grid=(size, groups),
        in_specs=in_specs,
        out_specs=[
            pl.BlockSpec((rows, n), lambda i, g: ((i + start) * groups + g, 0)),
            pl.BlockSpec(
                (fac_count, loc_count, 1, per_fac, GROUP, n), lambda i, g: (0, 0, i, 0, g, 0)
            ),
            pl.BlockSpec((1, GROUP, n), lambda i, g: (i, g, 0)),
        ],
        out_shape=[
            jax.ShapeDtypeStruct(cost.shape, jnp.float32),
            jax.ShapeDtypeStruct(
                (fac_count, loc_count, size, per_fac, loc_rows, n), jnp.float32
            ),
            jax.ShapeDtypeStruct((size, loc_rows, n), jnp.float32),
        ],
        scratch_shapes=[
            pltpu.VMEM((n, GROUP, n), jnp.float32),
            pltpu.VMEM((n, GROUP, n), jnp.float32),
        ],
        input_output_aliases=aliases,
        compiler_params=pltpu.CompilerParams(vmem_limit_bytes=24 * 1024 * 1024),
        cost_estimate=pl.CostEstimate(
            flops=elements * 40, bytes_accessed=elements * 12, transcendentals=elements * 6
        ),
        name="sweeps",
    )(*operands)


def join_kernel(sizes, pad, *refs):
    parts = refs[: len(sizes)]
    r_ref, o_ref, s_ref = refs[len(sizes):]
    fac_step, loc_count = parts[0].shape[0], parts[0].shape[1]
    width, rows = r_ref.shape[1], r_ref.shape[2]
    at = 0
    for f in range(fac_step):
        for part, size in zip(parts, sizes):
            for i in range(size):
                tile = jnp.concatenate([part[f, b, i, 0] for b in range(loc_count)], axis=0)
                s_ref[pl.ds(at * pad, tile.shape[1]), :] = tile.T
                at += 1

    for t in range(loc_count):

        def step(l, carry, t=t):
            partner = s_ref[pl.ds(t * width + l, rows, stride=pad), :]
            o_ref[t, l] = 0.5 * (r_ref[t, l] + partner)
            return carry

        lax.fori_loop(0, width, step, 0, unroll=8)


def join_chunks(reduced, parts, sizes, fac_rows, loc_rows, fac_count, loc_count):
    n = reduced.shape[2]
    fac_step = max(1, 8 // fac_rows)
    rows = fac_step * fac_rows
    per_fac = fac_rows // loc_count
    pad = n + 8
    own = pl.BlockSpec((loc_count, loc_rows, rows, n), lambda q, f: (q, 0, f, 0))
    return pl.pallas_call(
        functools.partial(join_kernel, sizes, pad),
        grid=(per_fac, fac_count // fac_step),
        in_specs=[
            pl.BlockSpec(
                (fac_step, loc_count, size, 1, loc_rows, n), lambda q, f: (f, 0, 0, q, 0, 0)
            )
            for size in sizes
        ]
        + [own],
        out_specs=own,
        out_shape=jax.ShapeDtypeStruct(reduced.shape, jnp.float32),
        scratch_shapes=[pltpu.VMEM((rows * pad, n), jnp.float32)],
        compiler_params=pltpu.CompilerParams(vmem_limit_bytes=24 * 1024 * 1024),
        cost_estimate=pl.CostEstimate(
            flops=reduced.size * 4, bytes_accessed=reduced.size * 12, transcendentals=0
        ),
        name="join",
    )(*parts, reduced)


def chunk_sizes(rows):
    sizes, left, size = [], rows, 1
    while left > 2 * size + 1:
        sizes.append(size)
        left -= size
        size *= 2
    return tuple(sizes) + (left,)


def on_device(quad_cost, leader):
    fac_rows, loc_rows, n, _ = quad_cost.shape
    fac_count = lax.axis_size("fac")
    loc_count = lax.axis_size("loc")
    flat = quad_cost.reshape(fac_rows * loc_rows * n, n)
    sizes = chunk_sizes(fac_rows)
    reduced, start = None, 0
    parts, worths = [], []
    for size in sizes:
        reduced, outgoing, worth = sweep_chunk(
            flat, reduced, start, size, fac_rows, loc_rows, fac_count, loc_count
        )
        shape = outgoing.shape
        outgoing = outgoing.reshape((fac_count * loc_count,) + shape[2:])
        incoming = lax.all_to_all(outgoing, ("fac", "loc"), split_axis=0, concat_axis=0, tiled=True)
        parts.append(incoming.reshape(shape))
        worths.append(worth[:, :, 0])
        start += size
    new_cost = join_chunks(
        reduced.reshape(quad_cost.shape), parts, sizes, fac_rows, loc_rows, fac_count, loc_count
    )
    leader = leader + jnp.concatenate(worths, axis=0)
    highest, totals = combined_all(partial_totals(leader, 1), "loc", join_totals)
    leader = leader - (-leader_temper * (highest + jnp.log(totals)))[:, None]
    highest, totals = combined_all(partial_totals(leader, 0), "fac", join_totals)
    leader = leader - (-leader_temper * (highest + jnp.log(totals)))[None, :]
    return (new_cost, leader)


def solution(mesh):
    return jax.shard_map(
        on_device,
        mesh=mesh,
        in_specs=(P("fac", "loc", None, None), P("fac", "loc")),
        out_specs=(P("fac", "loc", None, None), P("fac", "loc")),
        check_vma=False,
    )
```
